256 devices in a mesh: gx: 8 (over x, core), gy: 32 (over z, y).
Axes of the slice: x: 4, y: 4, z: 8, core: 2. Of those that a mesh axis runs over, the one named last changes fastest.
Arguments:
- fields: bfloat16 [4, 2, 6144, 8192], P(None, None, 'gx', 'gy'), may hold values from -6 to 6
- parent: float32 [4, 2, 48, 48], replicated, may hold values from -6 to 6
- rate: float32 [4, 2], replicated, may hold values from 0.3 to 3
Outputs:
- tendency: bfloat16 [4, 2, 6144, 8192], P(None, None, 'gx', 'gy')
- spectra: float32 [4, 2, 48, 48], replicated
The draws below stay inside these ranges and needn't reach their ends.
All inputs are finite; a program needn't handle non-finite values.
Results may differ from the reference program's by a relative error of at most 0.015.
Values may be sent and summed in bfloat16 or wider, within the bound.
No kernel may reach another device: no remote copies, remote signals or barrier semaphores. Data moves between devices by JAX's collectives and lax.ppermute only.
A program may use at most 64 MiB of HBM per device.

```python
import math
import jax
import jax.numpy as jnp
from jax import lax

F = 4
KW = 24
LEV = 2
NX = 6144
NY = 8192


def shard_levels(own_key, dims, cuts, least, top_value):
    factor_of = 1.0
    for position, shards_of in cuts:
        heights = jax.random.uniform(jax.random.fold_in(jax.random.fold_in(own_key, 6), position), (shards_of,), jnp.float32, least / len(cuts), top_value / len(cuts))
        factor_of = factor_of * jnp.repeat(jnp.exp(heights), dims[position] // shards_of).reshape((-1,) + (1,) * (len(dims) - 1 - position))
    return factor_of


def centred(stream_key, shape, spread, limit, split=(), held_as=jnp.bfloat16):
    loudness = shard_levels(stream_key, shape, split, -0.22, 0.18) if split else 1.0
    values = jax.random.normal(stream_key, shape, jnp.float32) * spread * loudness
    return jnp.minimum(jnp.maximum(values, -limit), limit).astype(held_as)


def setup_inputs(seed: int = 0) -> dict:
    streams_of = jax.random.split(jax.random.key(seed), 4)
    fields = centred(streams_of[0], (F, LEV, NX, NY), 1.0, 6.0, ((2, 8), (3, 32)))
    parent = centred(streams_of[1], (F, LEV, 2 * KW, 2 * KW), 1.0, 6.0, (), jnp.float32)
    rate = jnp.clip(jnp.exp(jax.random.uniform(streams_of[2], (F, LEV), jnp.float32, math.log(0.3), math.log(3.0))), 0.3, 3.0)
    return dict(fields=fields, parent=parent, rate=rate)


def basis(start, count, total):
    positions = start + jnp.arange(count, dtype=jnp.int32)
    modes = jnp.arange(2 * KW, dtype=jnp.int32)
    wavenum = jnp.where(modes < KW, modes, modes - KW + 1)
    phase = (positions[:, None] * wavenum[None, :] % total).astype(jnp.float32) * (2.0 * math.pi / total)
    return jnp.where(modes[None, :] < KW, jnp.cos(phase), jnp.sin(phase))

def reference(fields, parent, rate):
    flat = fields.reshape(F * LEV, NX, NY)
    x_table = basis(0, NX, NX)
    x_narrow = x_table.astype(jnp.bfloat16)
    y_table = basis(0, NY, NY)

    def analyse(single):
        x_coeffs = jnp.dot(x_narrow.T, single, preferred_element_type=jnp.float32)
        return jnp.dot(x_coeffs, y_table, precision=lax.Precision.HIGHEST)
    totals = lax.map(analyse, flat)
    spectra = 2.0 / math.sqrt(NX * NY) * totals.reshape(F, LEV, 2 * KW, 2 * KW)
    delta = rate[:, :, None, None] * (parent - spectra)

    def synthesize(single):
        across = jnp.dot(single, y_table.T, precision=lax.Precision.HIGHEST)
        whole = jnp.dot(x_table, across, precision=lax.Precision.HIGHEST)
        return (whole / (2 * KW)).astype(jnp.bfloat16)
    tendency = lax.map(synthesize, delta.reshape(F * LEV, 2 * KW, 2 * KW))
    return (tendency.reshape(F, LEV, NX, NY), spectra)
```

```python
import math

import jax
import jax.numpy as jnp
import ml_dtypes
import numpy as np
from jax import lax
from jax.experimental import pallas as pl
from jax.experimental.pallas import tpu as pltpu
from jax.sharding import Mesh
from jax.sharding import PartitionSpec as P

KW = 24
MODES = 2 * KW
FLAT = 8
PIECE = 16
WIDTH = 3 * FLAT * PIECE
AXES = ("x", "c", "z", "y")
SIZES = {"x": 4, "c": 2, "z": 8, "y": 4}
CHIPS = [(x, y, z) for x in range(4) for y in range(4) for z in range(8)]


def basis(total):
    positions = np.arange(total, dtype=np.int64)
    modes = np.arange(MODES)
    wavenum = np.where(modes < KW, modes, modes - KW + 1)
    phase = (positions[:, None] * wavenum[None, :] % total) * (2.0 * math.pi / total)
    return np.where(modes[None, :] < KW, np.cos(phase), np.sin(phase)).astype(np.float32)


def halves(table):
    high = table.astype(ml_dtypes.bfloat16)
    low = (table - high.astype(np.float32)).astype(ml_dtypes.bfloat16)
    return high, low


def index_of(x, c, z, y):
    return ((x * 2 + c) * 8 + z) * 4 + y


def swap_cores():
    return [
        (index_of(x, c, z, y), index_of(x, 1 - c, z, y)) for x, y, z in CHIPS for c in (0, 1)
    ]


def hand_over(core, move):
    pairs = []
    for x, y, z in CHIPS:
        to_x, to_y, to_z = move(x, y, z)
        pairs.append((index_of(x, core, z, y), index_of(to_x, 1 - core, to_z, to_y)))
        pairs.append((index_of(x, 1 - core, z, y), index_of(x, core, z, y)))
    return pairs


def both(first, second):
    return lambda x, y, z: second(*first(x, y, z))


FLIP_X0 = lambda x, y, z: (x ^ 1, y, z)
FLIP_X1 = lambda x, y, z: (3 - x, y, z)
FLIP_Y0 = lambda x, y, z: (x, y ^ 1, z)
FLIP_Y1 = lambda x, y, z: (x, 3 - y, z)
FLIP_Z0 = lambda x, y, z: (x, y, z ^ 1)
FLIP_Z1 = lambda x, y, z: (x, y, z ^ 2)
FLIP_Z2 = lambda x, y, z: (x, y, 7 - z)
STAGES = ((FLIP_X0, FLIP_Y0), (FLIP_Z0, FLIP_Z1), (FLIP_X1, FLIP_Y1), (FLIP_Z2,))


def total_of(partial):
    core = 1
    half = partial.astype(jnp.bfloat16)
    running = half.astype(jnp.float32) + lax.ppermute(half, AXES, swap_cores()).astype(jnp.float32)
    for stage in STAGES:
        value = running.astype(jnp.bfloat16)
        moves = stage if len(stage) == 1 else (*stage, both(*stage))
        near = [lax.ppermute(value, AXES, hand_over(core, move)) for move in moves]
        own = lax.ppermute(value, AXES, swap_cores()).astype(jnp.float32)
        near = [part.astype(jnp.float32) for part in near]
        if len(near) == 1:
            running = own + near[0]
        else:
            running = (own + near[0]) + (near[1] + near[2])
        core = 1 - core
    other = lax.ppermute(running, AXES, swap_cores())
    return jnp.where(lax.axis_index("c") == core, running, other)


def mask_of(flat, rows):
    lane = lax.broadcasted_iota(jnp.int32, (rows, WIDTH), 1)
    return lane // PIECE % FLAT == flat


def dot(a, b, dims=((1,), (0,))):
    return lax.dot_general(a, b, (dims, ((), ())), preferred_element_type=jnp.float32)


def split(value):
    high = value.astype(jnp.bfloat16)
    return high, (value - high.astype(jnp.float32)).astype(jnp.bfloat16)


def where_am_i():
    gx = lax.axis_index("x") * 2 + lax.axis_index("c")
    gy = lax.axis_index("z") * 4 + lax.axis_index("y")
    return gx, gy


def analyse(scale, fields, x_tables, y_tables, out, blocks, x_table, y_table, high, low, sems):
    gx, gy = where_am_i()
    copy_y = pltpu.make_async_copy(y_tables.at[gy], y_table, sems.at[FLAT])
    copy_x = pltpu.make_async_copy(x_tables.at[gx], x_table, sems.at[FLAT + 1])
    copies = [
        pltpu.make_async_copy(fields.at[f // 2, f % 2], blocks.at[f], sems.at[f])
        for f in range(FLAT)
    ]
    copy_x.start()
    copies[0].start()
    copy_y.start()
    for copy in copies[1:]:
        copy.start()
    copy_x.wait()
    for f in range(FLAT):
        copies[f].wait()
        high[pl.ds(f * MODES, MODES)], low[pl.ds(f * MODES, MODES)] = split(
            dot(x_table[...], blocks[f])
        )
    copy_y.wait()
    row = lax.broadcasted_iota(jnp.int32, (WIDTH, MODES), 0)
    mode = lax.broadcasted_iota(jnp.int32, (WIDTH, MODES), 1)
    spread = (row // 128 * PIECE + row % PIECE == mode).astype(jnp.bfloat16)
    y_high = dot(spread, y_table[:MODES]).astype(jnp.bfloat16)
    y_low = dot(spread, y_table[MODES:]).astype(jnp.bfloat16)
    last = ((1,), (1,))
    product = (
        dot(high[...], y_high, last) + dot(low[...], y_high, last) + dot(high[...], y_low, last)
    )
    total = jnp.zeros((MODES, WIDTH), jnp.float32)
    for f in range(FLAT):
        total = jnp.where(mask_of(f, MODES), product[f * MODES : (f + 1) * MODES], total)
    out[...] = total * scale


def synthesise(sums, parent, rate, x_tables, y_tables, out, spectra, blocks, x_table, y_table, sems):
    gx, gy = where_am_i()
    copy_y = pltpu.make_async_copy(y_tables.at[gy], y_table, sems.at[FLAT])
    copy_x = pltpu.make_async_copy(x_tables.at[gx], x_table, sems.at[FLAT + 1])
    copy_y.start()
    copy_x.start()
    high, low = split(sums[...])
    none = jnp.zeros((MODES, WIDTH), jnp.bfloat16)
    highs = jnp.concatenate([jnp.where(mask_of(f, MODES), high, none) for f in range(FLAT)])
    lows = jnp.concatenate([jnp.where(mask_of(f, MODES), low, none) for f in range(FLAT)])
    row = lax.broadcasted_iota(jnp.int32, (WIDTH, MODES), 0)
    mode = lax.broadcasted_iota(jnp.int32, (WIDTH, MODES), 1)
    gather = (row // 128 * PIECE + row % PIECE == mode).astype(jnp.bfloat16)
    coeffs = dot(highs, gather) + dot(lows, gather)
    copy_y.wait()
    y_high, y_low = y_table[:MODES], y_table[MODES:]
    rows = []
    for f in range(FLAT):
        mine = coeffs[f * MODES : (f + 1) * MODES]
        spectra[f // 2, f % 2] = mine
        rows.append((rate[f // 2, f % 2] / MODES) * (parent[f // 2, f % 2] - mine))
    d_high, d_low = split(jnp.concatenate(rows))
    across = dot(d_high, y_high) + dot(d_low, y_high) + dot(d_high, y_low)
    a_high, a_low = split(across)
    copy_x.wait()
    copies = []
    for f in range(FLAT):
        mine = slice(f * MODES, (f + 1) * MODES)
        weights = jnp.concatenate([a_high[mine], a_high[mine], a_low[mine]])
        blocks[f] = dot(x_table[...], weights).astype(jnp.bfloat16)
        copy = pltpu.make_async_copy(blocks.at[f], out.at[f // 2, f % 2], sems.at[f])
        copy.start()
        copies.append(copy)
    for copy in copies:
        copy.wait()


def solution(mesh):
    fine = Mesh(mesh.devices.reshape(tuple(SIZES[a] for a in AXES)), AXES)
    total_x, total_y = 6144, 8192
    cols_x, cols_y = total_x // 8, total_y // 32
    x_high, x_low = halves(basis(total_x))
    y_high, y_low = halves(basis(total_y))
    narrow = x_high.reshape(8, cols_x, MODES).transpose(0, 2, 1)
    x_tables = np.concatenate([x_high, x_low, x_high], 1).reshape(8, cols_x, 3 * MODES)
    y_tables = np.concatenate(
        [t.reshape(32, cols_y, MODES).transpose(0, 2, 1) for t in (y_high, y_low)], 1
    )
    scale = 2.0 / math.sqrt(total_x * total_y)
    any_space = pl.BlockSpec(memory_space=pl.ANY)
    vmem = pl.BlockSpec(memory_space=pltpu.VMEM)
    grant = pltpu.CompilerParams(vmem_limit_bytes=24 * 1024 * 1024)

    def per_device(fields, parent, rate):
        partial = pl.pallas_call(
            lambda *refs: analyse(scale, *refs),
            out_shape=jax.ShapeDtypeStruct((MODES, WIDTH), jnp.float32),
            in_specs=[any_space] * 3,
            out_specs=vmem,
            scratch_shapes=[
                pltpu.VMEM((FLAT, cols_x, cols_y), jnp.bfloat16),
                pltpu.VMEM((MODES, cols_x), jnp.bfloat16),
                pltpu.VMEM((2 * MODES, cols_y), jnp.bfloat16),
                pltpu.VMEM((FLAT * MODES, cols_y), jnp.bfloat16),
                pltpu.VMEM((FLAT * MODES, cols_y), jnp.bfloat16),
                pltpu.SemaphoreType.DMA((FLAT + 2,)),
            ],
            compiler_params=grant,
            name="analyse",
        )(fields, jnp.asarray(narrow), jnp.asarray(y_tables))
        with jax.named_scope("total"):
            sums = total_of(partial)
        tendency, spectra = pl.pallas_call(
            synthesise,
            out_shape=(
                jax.ShapeDtypeStruct((4, 2, cols_x, cols_y), jnp.bfloat16),
                jax.ShapeDtypeStruct((4, 2, MODES, MODES), jnp.float32),
            ),
            in_specs=[vmem, vmem, pl.BlockSpec(memory_space=pltpu.SMEM), any_space, any_space],
            out_specs=(any_space, vmem),
            scratch_shapes=[
                pltpu.VMEM((FLAT, cols_x, cols_y), jnp.bfloat16),
                pltpu.VMEM((cols_x, 3 * MODES), jnp.bfloat16),
                pltpu.VMEM((2 * MODES, cols_y), jnp.bfloat16),
                pltpu.SemaphoreType.DMA((FLAT + 2,)),
            ],
            compiler_params=grant,
            name="synthesise",
        )(sums, parent, rate, jnp.asarray(x_tables), jnp.asarray(y_tables))
        return tendency, spectra

    grid = P(None, None, ("x", "c"), ("z", "y"))
    return jax.shard_map(
        per_device, mesh=fine, in_specs=(grid, P(), P()), out_specs=(grid, P()), check_vma=False
    )
```

```python
import math

import jax
import jax.numpy as jnp
import ml_dtypes
import numpy as np
from jax import lax
from jax.experimental import pallas as pl
from jax.experimental.pallas import tpu as pltpu
from jax.sharding import Mesh
from jax.sharding import PartitionSpec as P

KW = 24
MODES = 2 * KW
FLAT = 8
PIECE = 16
WIDTH = 3 * FLAT * PIECE
AXES = ("x", "c", "z", "y")
SIZES = {"x": 4, "c": 2, "z": 8, "y": 4}
CHIPS = [(x, y, z) for x in range(4) for y in range(4) for z in range(8)]


def basis(total):
    positions = np.arange(total, dtype=np.int64)
    modes = np.arange(MODES)
    wavenum = np.where(modes < KW, modes, modes - KW + 1)
    phase = (positions[:, None] * wavenum[None, :] % total) * (2.0 * math.pi / total)
    return np.where(modes[None, :] < KW, np.cos(phase), np.sin(phase)).astype(np.float32)


def halves(table):
    high = table.astype(ml_dtypes.bfloat16)
    low = (table - high.astype(np.float32)).astype(ml_dtypes.bfloat16)
    return high, low


def index_of(x, c, z, y):
    return ((x * 2 + c) * 8 + z) * 4 + y


def swap_cores():
    return [
        (index_of(x, c, z, y), index_of(x, 1 - c, z, y)) for x, y, z in CHIPS for c in (0, 1)
    ]


def hand_over(core, move):
    pairs = []
    for x, y, z in CHIPS:
        to_x, to_y, to_z = move(x, y, z)
        pairs.append((index_of(x, core, z, y), index_of(to_x, 1 - core, to_z, to_y)))
        pairs.append((index_of(x, 1 - core, z, y), index_of(x, core, z, y)))
    return pairs


def both(first, second):
    return lambda x, y, z: second(*first(x, y, z))


FLIP_X0 = lambda x, y, z: (x ^ 1, y, z)
FLIP_X1 = lambda x, y, z: (3 - x, y, z)
FLIP_Y0 = lambda x, y, z: (x, y ^ 1, z)
FLIP_Y1 = lambda x, y, z: (x, 3 - y, z)
FLIP_Z0 = lambda x, y, z: (x, y, z ^ 1)
FLIP_Z1 = lambda x, y, z: (x, y, z ^ 2)
FLIP_Z2 = lambda x, y, z: (x, y, 7 - z)
STAGES = ((FLIP_X1, FLIP_Y1), (FLIP_Z1, FLIP_Z2), (FLIP_Y0, FLIP_Z0))
LAST = FLIP_X0


def on_both(move):
    pairs = []
    for x, y, z in CHIPS:
        to_x, to_y, to_z = move(x, y, z)
        pairs += [(index_of(x, c, z, y), index_of(to_x, c, to_z, to_y)) for c in (0, 1)]
    return pairs


def total_of(half):
    core = 0
    running = half.astype(jnp.float32) + lax.ppermute(half, AXES, swap_cores()).astype(jnp.float32)
    for stage in STAGES:
        value = running.astype(jnp.bfloat16)
        near = [
            lax.ppermute(value, AXES, hand_over(core, move)).astype(jnp.float32)
            for move in (*stage, both(*stage))
        ]
        own = lax.ppermute(value, AXES, swap_cores()).astype(jnp.float32)
        running = (own + near[0]) + (near[1] + near[2])
        core = 1 - core
    value = running.astype(jnp.bfloat16)
    crossed = lax.ppermute(value, AXES, hand_over(core, LAST))
    straight = lax.ppermute(value, AXES, on_both(LAST))
    own = lax.ppermute(value, AXES, swap_cores())
    holds = lax.axis_index("c") == core
    own = jnp.where(holds, value, own).astype(jnp.float32)
    return own + jnp.where(holds, straight, crossed).astype(jnp.float32)


def mask_of(flat, rows):
    lane = lax.broadcasted_iota(jnp.int32, (rows, WIDTH), 1)
    return lane // PIECE % FLAT == flat


def dot(a, b, dims=((1,), (0,))):
    return lax.dot_general(a, b, (dims, ((), ())), preferred_element_type=jnp.float32)


def split(value):
    high = value.astype(jnp.bfloat16)
    return high, (value - high.astype(jnp.float32)).astype(jnp.bfloat16)


def where_am_i():
    gx = lax.axis_index("x") * 2 + lax.axis_index("c")
    gy = lax.axis_index("z") * 4 + lax.axis_index("y")
    return gx, gy


def analyse(
    scale, fields, x_tables, y_tables, x_wides, out, x_wide, y_table, blocks, x_table, high, low, sems
):
    gx, gy = where_am_i()
    copy_y = pltpu.make_async_copy(y_tables.at[gy, pl.ds(0, 2 * MODES)], y_table, sems.at[FLAT])
    copy_x = pltpu.make_async_copy(x_tables.at[gx, pl.ds(0, MODES)], x_table, sems.at[FLAT + 1])
    copy_wide = pltpu.make_async_copy(x_wides.at[gx], x_wide, sems.at[FLAT + 2])
    copies = [
        pltpu.make_async_copy(fields.at[f // 2, f % 2], blocks.at[f], sems.at[f])
        for f in range(FLAT)
    ]
    copies[0].start()
    copy_x.start()
    copy_y.start()
    for copy in copies[1:]:
        copy.start()
    copy_wide.start()
    copy_y.wait()
    row = lax.broadcasted_iota(jnp.int32, (WIDTH, MODES), 0)
    mode = lax.broadcasted_iota(jnp.int32, (WIDTH, MODES), 1)
    spread = (row // 128 * PIECE + row % PIECE == mode).astype(jnp.bfloat16)
    y_high = dot(spread, y_table[:MODES]).astype(jnp.bfloat16)
    y_low = dot(spread, y_table[MODES:]).astype(jnp.bfloat16)
    copy_x.wait()
    for pair in range(0, FLAT, 2):
        copies[pair].wait()
        copies[pair + 1].wait()
        for f in (pair, pair + 1):
            mine = pl.ds(f * MODES, MODES)
            high[mine], low[mine] = split(dot(x_table[...], blocks[f]))
    last = ((1,), (1,))
    product = (
        dot(high[...], y_high, last) + dot(low[...], y_high, last) + dot(high[...], y_low, last)
    )
    total = jnp.zeros((MODES, WIDTH), jnp.float32)
    for f in range(FLAT):
        total = jnp.where(mask_of(f, MODES), product[f * MODES : (f + 1) * MODES], total)
    out[...] = (total * scale).astype(jnp.bfloat16)
    copy_wide.wait()


def synthesise(sums, parent, rate, x_table, y_table, out, spectra, blocks, sems):
    high, low = split(sums[...])
    none = jnp.zeros((MODES, WIDTH), jnp.bfloat16)
    highs = jnp.concatenate([jnp.where(mask_of(f, MODES), high, none) for f in range(FLAT)])
    lows = jnp.concatenate([jnp.where(mask_of(f, MODES), low, none) for f in range(FLAT)])
    row = lax.broadcasted_iota(jnp.int32, (WIDTH, MODES), 0)
    mode = lax.broadcasted_iota(jnp.int32, (WIDTH, MODES), 1)
    gather = (row // 128 * PIECE + row % PIECE == mode).astype(jnp.bfloat16)
    coeffs = dot(highs, gather) + dot(lows, gather)
    y_high, y_low = y_table[:MODES], y_table[MODES:]
    rows = []
    for f in range(FLAT):
        mine = coeffs[f * MODES : (f + 1) * MODES]
        spectra[f // 2, f % 2] = mine
        rows.append((rate[f // 2, f % 2] / MODES) * (parent[f // 2, f % 2] - mine))
    d_high, d_low = split(jnp.concatenate(rows))
    across = dot(d_high, y_high) + dot(d_low, y_high) + dot(d_high, y_low)
    a_high, a_low = split(across)
    copies = []
    for f in range(FLAT):
        mine = slice(f * MODES, (f + 1) * MODES)
        weights = jnp.concatenate([a_high[mine], a_high[mine], a_low[mine]])
        blocks[f] = dot(x_table[...], weights).astype(jnp.bfloat16)
        copy = pltpu.make_async_copy(blocks.at[f], out.at[f // 2, f % 2], sems.at[f])
        copy.start()
        copies.append(copy)
    for copy in copies:
        copy.wait()


def solution(mesh):
    fine = Mesh(mesh.devices.reshape(tuple(SIZES[a] for a in AXES)), AXES)
    total_x, total_y = 6144, 8192
    cols_x, cols_y = total_x // 8, total_y // 32
    x_high, x_low = halves(basis(total_x))
    y_high, y_low = halves(basis(total_y))
    narrow = np.pad(x_high.reshape(8, cols_x, MODES).transpose(0, 2, 1), ((0, 0), (0, 208), (0, 0)))
    x_wides = np.concatenate([x_high, x_low, x_high], 1).reshape(8, cols_x, 3 * MODES)
    y_tables = np.concatenate(
        [t.reshape(32, cols_y, MODES).transpose(0, 2, 1) for t in (y_high, y_low)], 1
    )
    y_tables = np.pad(y_tables, ((0, 0), (0, 96), (0, 0)))
    scale = 2.0 / math.sqrt(total_x * total_y)
    any_space = pl.BlockSpec(memory_space=pl.ANY)
    vmem = pl.BlockSpec(memory_space=pltpu.VMEM)
    small = jax.ShapeDtypeStruct((MODES, WIDTH), jnp.bfloat16)

    def per_device(fields, parent, rate):
        partial, x_wide, y_table = pl.pallas_call(
            lambda *refs: analyse(scale, *refs),
            out_shape=(
                small,
                jax.ShapeDtypeStruct((cols_x, 3 * MODES), jnp.bfloat16),
                jax.ShapeDtypeStruct((2 * MODES, cols_y), jnp.bfloat16),
            ),
            in_specs=[any_space] * 4,
            out_specs=(vmem, vmem, vmem),
            scratch_shapes=[
                pltpu.VMEM((FLAT, cols_x, cols_y), jnp.bfloat16),
                pltpu.VMEM((MODES, cols_x), jnp.bfloat16),
                pltpu.VMEM((FLAT * MODES, cols_y), jnp.bfloat16),
                pltpu.VMEM((FLAT * MODES, cols_y), jnp.bfloat16),
                pltpu.SemaphoreType.DMA((FLAT + 3,)),
            ],
            compiler_params=pltpu.CompilerParams(vmem_limit_bytes=52 << 20),
            name="analyse",
        )(fields, jnp.asarray(narrow), jnp.asarray(y_tables), jnp.asarray(x_wides))
        with jax.named_scope("total"):
            sums = total_of(partial)
        return pl.pallas_call(
            synthesise,
            out_shape=(
                jax.ShapeDtypeStruct((4, 2, cols_x, cols_y), jnp.bfloat16),
                jax.ShapeDtypeStruct((4, 2, MODES, MODES), jnp.float32),
            ),
            in_specs=[vmem, vmem, pl.BlockSpec(memory_space=pltpu.SMEM), vmem, vmem],
            out_specs=(any_space, vmem),
            scratch_shapes=[
                pltpu.VMEM((FLAT, cols_x, cols_y), jnp.bfloat16),
                pltpu.SemaphoreType.DMA((FLAT,)),
            ],
            compiler_params=pltpu.CompilerParams(vmem_limit_bytes=16 << 20),
            name="synthesise",
        )(sums, parent, rate, x_wide, y_table)

    grid = P(None, None, ("x", "c"), ("z", "y"))
    return jax.shard_map(
        per_device, mesh=fine, in_specs=(grid, P(), P()), out_specs=(grid, P()), check_vma=False
    )
```

```python
import math

import jax
import jax.numpy as jnp
import ml_dtypes
import numpy as np
from jax import lax
from jax.experimental import pallas as pl
from jax.experimental.pallas import tpu as pltpu
from jax.sharding import Mesh
from jax.sharding import PartitionSpec as P

KW = 24
MODES = 2 * KW
FLAT = 8
WIDTH = FLAT * MODES
SPECTRA_AFTER = 3
AXES = ("x", "c", "z", "y")
SIZES = {"x": 4, "c": 2, "z": 8, "y": 4}
CHIPS = [(x, y, z) for x in range(4) for y in range(4) for z in range(8)]


def basis(total):
    positions = np.arange(total, dtype=np.int64)
    modes = np.arange(MODES)
    wavenum = np.where(modes < KW, modes, modes - KW + 1)
    phase = (positions[:, None] * wavenum[None, :] % total) * (2.0 * math.pi / total)
    return np.where(modes[None, :] < KW, np.cos(phase), np.sin(phase)).astype(np.float32)


def halves(table):
    high = table.astype(ml_dtypes.bfloat16)
    low = (table - high.astype(np.float32)).astype(ml_dtypes.bfloat16)
    return high, low


def index_of(x, c, z, y):
    return ((x * 2 + c) * 8 + z) * 4 + y


def swap_cores():
    return [
        (index_of(x, c, z, y), index_of(x, 1 - c, z, y)) for x, y, z in CHIPS for c in (0, 1)
    ]


def hand_over(core, move):
    pairs = []
    for x, y, z in CHIPS:
        to_x, to_y, to_z = move(x, y, z)
        pairs.append((index_of(x, core, z, y), index_of(to_x, 1 - core, to_z, to_y)))
        pairs.append((index_of(x, 1 - core, z, y), index_of(x, core, z, y)))
    return pairs


def both(first, second):
    return lambda x, y, z: second(*first(x, y, z))


FLIP_X0 = lambda x, y, z: (x ^ 1, y, z)
FLIP_X1 = lambda x, y, z: (3 - x, y, z)
FLIP_Y0 = lambda x, y, z: (x, y ^ 1, z)
FLIP_Y1 = lambda x, y, z: (x, 3 - y, z)
FLIP_Z0 = lambda x, y, z: (x, y, z ^ 1)
FLIP_Z1 = lambda x, y, z: (x, y, z ^ 2)
FLIP_Z2 = lambda x, y, z: (x, y, 7 - z)
STAGES = ((FLIP_X0, FLIP_Y0), (FLIP_Z0, FLIP_Z1), (FLIP_X1, FLIP_Y1))
LAST = FLIP_Z2


def on_both(move):
    pairs = []
    for x, y, z in CHIPS:
        to_x, to_y, to_z = move(x, y, z)
        pairs += [(index_of(x, c, z, y), index_of(to_x, c, to_z, to_y)) for c in (0, 1)]
    return pairs


def total_of(half):
    core = 0
    running = half.astype(jnp.float32) + lax.ppermute(half, AXES, swap_cores()).astype(jnp.float32)
    for stage in STAGES:
        value = running.astype(jnp.bfloat16)
        near = [
            lax.ppermute(value, AXES, hand_over(core, move)).astype(jnp.float32)
            for move in (*stage, both(*stage))
        ]
        own = lax.ppermute(value, AXES, swap_cores()).astype(jnp.float32)
        running = (own + near[0]) + (near[1] + near[2])
        core = 1 - core
    value = running.astype(jnp.bfloat16)
    crossed = lax.ppermute(value, AXES, hand_over(core, LAST))
    straight = lax.ppermute(value, AXES, on_both(LAST))
    own = lax.ppermute(value, AXES, swap_cores())
    holds = lax.axis_index("c") == core
    own = jnp.where(holds, value, own).astype(jnp.float32)
    return own + jnp.where(holds, straight, crossed).astype(jnp.float32)


def mask_of(flat, rows):
    lane = lax.broadcasted_iota(jnp.int32, (rows, WIDTH), 1)
    return (lane >= flat * MODES) & (lane < (flat + 1) * MODES)


def dot(a, b, dims=((1,), (0,))):
    return lax.dot_general(a, b, (dims, ((), ())), preferred_element_type=jnp.float32)


def split(value):
    high = value.astype(jnp.bfloat16)
    return high, (value - high.astype(jnp.float32)).astype(jnp.bfloat16)


def where_am_i():
    gx = lax.axis_index("x") * 2 + lax.axis_index("c")
    gy = lax.axis_index("z") * 4 + lax.axis_index("y")
    return gx, gy


def analyse(
    scale, fields, x_tables, y_tables, x_wides, out, x_wide, y_table, blocks, x_table, high, low, sems
):
    gx, gy = where_am_i()
    copy_y = pltpu.make_async_copy(y_tables.at[gy, pl.ds(0, 2 * MODES)], y_table, sems.at[FLAT])
    copy_x = pltpu.make_async_copy(x_tables.at[gx, pl.ds(0, MODES)], x_table, sems.at[FLAT + 1])
    copy_wide = pltpu.make_async_copy(x_wides.at[gx], x_wide, sems.at[FLAT + 2])
    copies = [
        pltpu.make_async_copy(fields.at[f // 2, f % 2], blocks.at[f], sems.at[f])
        for f in range(FLAT)
    ]
    copies[0].start()
    copy_x.start()
    copy_y.start()
    for copy in copies[1:]:
        copy.start()
    copy_wide.start()
    copy_y.wait()
    y_high = jnp.concatenate([y_table[:MODES]] * FLAT)
    y_low = jnp.concatenate([y_table[MODES:]] * FLAT)
    copy_x.wait()
    for pair in range(0, FLAT, 2):
        copies[pair].wait()
        copies[pair + 1].wait()
        for f in (pair, pair + 1):
            mine = pl.ds(f * MODES, MODES)
            high[mine], low[mine] = split(dot(x_table[...], blocks[f]))
    last = ((1,), (1,))
    product = (
        dot(high[...], y_high, last) + dot(low[...], y_high, last) + dot(high[...], y_low, last)
    )
    total = jnp.zeros((MODES, WIDTH), jnp.float32)
    for f in range(FLAT):
        total = jnp.where(mask_of(f, MODES), product[f * MODES : (f + 1) * MODES], total)
    out[...] = (total * scale).astype(jnp.bfloat16)
    copy_wide.wait()


def synthesise(sums, parent, rate, x_table, y_table, out, spectra, blocks, modes, sems):
    y_high, y_low = y_table[:MODES], y_table[MODES:]
    p_high, p_low = split(jnp.concatenate([parent[f // 2, f % 2] for f in range(FLAT)]))
    wanted = dot(p_high, y_high) + dot(p_low, y_high) + dot(p_high, y_low)
    high, low = split(sums[...])
    none = jnp.zeros((MODES, WIDTH), jnp.bfloat16)
    highs = jnp.concatenate([jnp.where(mask_of(f, MODES), high, none) for f in range(FLAT)])
    lows = jnp.concatenate([jnp.where(mask_of(f, MODES), low, none) for f in range(FLAT)])
    y_high, y_low = jnp.concatenate([y_high] * FLAT), jnp.concatenate([y_low] * FLAT)
    found = dot(highs, y_high) + dot(lows, y_high) + dot(highs, y_low)
    row = lax.broadcasted_iota(jnp.int32, (WIDTH, MODES), 0)
    mode = lax.broadcasted_iota(jnp.int32, (WIDTH, MODES), 1)
    gather = (row % MODES == mode).astype(jnp.bfloat16)
    copies = []
    for f in range(FLAT):
        mine = slice(f * MODES, (f + 1) * MODES)
        pull = rate[f // 2 : f // 2 + 1, f % 2 : f % 2 + 1] / MODES
        a_high, a_low = split(pull * (wanted[mine] - found[mine]))
        weights = jnp.concatenate([a_high, a_high, a_low])
        blocks[f] = dot(x_table[...], weights).astype(jnp.bfloat16)
        copies.append(pltpu.make_async_copy(blocks.at[f], out.at[f // 2, f % 2], sems.at[f]))
        copies[-1].start()
        if f == SPECTRA_AFTER:
            coeffs = dot(highs, gather) + dot(lows, gather)
            for g in range(FLAT):
                modes[g // 2, g % 2] = coeffs[g * MODES : (g + 1) * MODES]
            copies.append(pltpu.make_async_copy(modes, spectra, sems.at[FLAT]))
            copies[-1].start()
    for copy in copies:
        copy.wait()


def solution(mesh):
    fine = Mesh(mesh.devices.reshape(tuple(SIZES[a] for a in AXES)), AXES)
    total_x, total_y = 6144, 8192
    cols_x, cols_y = total_x // 8, total_y // 32
    x_high, x_low = halves(basis(total_x))
    y_high, y_low = halves(basis(total_y))
    narrow = np.pad(x_high.reshape(8, cols_x, MODES).transpose(0, 2, 1), ((0, 0), (0, 208), (0, 0)))
    x_wides = np.concatenate([x_high, x_low, x_high], 1).reshape(8, cols_x, 3 * MODES)
    y_tables = np.concatenate(
        [t.reshape(32, cols_y, MODES).transpose(0, 2, 1) for t in (y_high, y_low)], 1
    )
    y_tables = np.pad(y_tables, ((0, 0), (0, 96), (0, 0)))
    scale = 2.0 / math.sqrt(total_x * total_y)
    any_space = pl.BlockSpec(memory_space=pl.ANY)
    vmem = pl.BlockSpec(memory_space=pltpu.VMEM)
    small = jax.ShapeDtypeStruct((MODES, WIDTH), jnp.bfloat16)

    def per_device(fields, parent, rate):
        partial, x_wide, y_table = pl.pallas_call(
            lambda *refs: analyse(scale, *refs),
            out_shape=(
                small,
                jax.ShapeDtypeStruct((cols_x, 3 * MODES), jnp.bfloat16),
                jax.ShapeDtypeStruct((2 * MODES, cols_y), jnp.bfloat16),
            ),
            in_specs=[any_space] * 4,
            out_specs=(vmem, vmem, vmem),
            scratch_shapes=[
                pltpu.VMEM((FLAT, cols_x, cols_y), jnp.bfloat16),
                pltpu.VMEM((MODES, cols_x), jnp.bfloat16),
                pltpu.VMEM((FLAT * MODES, cols_y), jnp.bfloat16),
                pltpu.VMEM((FLAT * MODES, cols_y), jnp.bfloat16),
                pltpu.SemaphoreType.DMA((FLAT + 3,)),
            ],
            compiler_params=pltpu.CompilerParams(vmem_limit_bytes=52 << 20),
            name="analyse",
        )(fields, jnp.asarray(narrow), jnp.asarray(y_tables), jnp.asarray(x_wides))
        with jax.named_scope("total"):
            sums = total_of(partial)
        return pl.pallas_call(
            synthesise,
            out_shape=(
                jax.ShapeDtypeStruct((4, 2, cols_x, cols_y), jnp.bfloat16),
                jax.ShapeDtypeStruct((4, 2, MODES, MODES), jnp.float32),
            ),
            in_specs=[vmem] * 5,
            out_specs=(any_space, any_space),
            scratch_shapes=[
                pltpu.VMEM((FLAT, cols_x, cols_y), jnp.bfloat16),
                pltpu.VMEM((4, 2, MODES, MODES), jnp.float32),
                pltpu.SemaphoreType.DMA((FLAT + 1,)),
            ],
            compiler_params=pltpu.CompilerParams(vmem_limit_bytes=16 << 20),
            name="synthesise",
        )(sums, parent, rate, x_wide, y_table)

    grid = P(None, None, ("x", "c"), ("z", "y"))
    return jax.shard_map(
        per_device, mesh=fine, in_specs=(grid, P(), P()), out_specs=(grid, P()), check_vma=False
    )
```

```python
import math

import jax
import jax.numpy as jnp
import ml_dtypes
import numpy as np
from jax import lax
from jax.experimental import pallas as pl
from jax.experimental.pallas import tpu as pltpu
from jax.sharding import Mesh
from jax.sharding import PartitionSpec as P

KW = 24
MODES = 2 * KW
FLAT = 8
WIDTH = FLAT * MODES
SPECTRA_AFTER = 3
AXES = ("x", "c", "z", "y")
SIZES = {"x": 4, "c": 2, "z": 8, "y": 4}
CHIPS = [(x, y, z) for x in range(4) for y in range(4) for z in range(8)]


def basis(total):
    positions = np.arange(total, dtype=np.int64)
    modes = np.arange(MODES)
    wavenum = np.where(modes < KW, modes, modes - KW + 1)
    phase = (positions[:, None] * wavenum[None, :] % total) * (2.0 * math.pi / total)
    return np.where(modes[None, :] < KW, np.cos(phase), np.sin(phase)).astype(np.float32)


def halves(table):
    high = table.astype(ml_dtypes.bfloat16)
    low = (table - high.astype(np.float32)).astype(ml_dtypes.bfloat16)
    return high, low


def index_of(x, c, z, y):
    return ((x * 2 + c) * 8 + z) * 4 + y


def swap_cores():
    return [
        (index_of(x, c, z, y), index_of(x, 1 - c, z, y)) for x, y, z in CHIPS for c in (0, 1)
    ]


def hand_over(core, move):
    pairs = []
    for x, y, z in CHIPS:
        to_x, to_y, to_z = move(x, y, z)
        pairs.append((index_of(x, core, z, y), index_of(to_x, 1 - core, to_z, to_y)))
        pairs.append((index_of(x, 1 - core, z, y), index_of(x, core, z, y)))
    return pairs


def both(first, second):
    return lambda x, y, z: second(*first(x, y, z))


FLIP_X0 = lambda x, y, z: (x ^ 1, y, z)
FLIP_X1 = lambda x, y, z: (3 - x, y, z)
FLIP_Y0 = lambda x, y, z: (x, y ^ 1, z)
FLIP_Y1 = lambda x, y, z: (x, 3 - y, z)
FLIP_Z0 = lambda x, y, z: (x, y, z ^ 1)
FLIP_Z1 = lambda x, y, z: (x, y, z ^ 2)
FLIP_Z2 = lambda x, y, z: (x, y, 7 - z)
STAGES = ((FLIP_X0, FLIP_Y0), (FLIP_Z0, FLIP_Z1), (FLIP_X1, FLIP_Y1))
LAST = FLIP_Z2


def on_both(move):
    pairs = []
    for x, y, z in CHIPS:
        to_x, to_y, to_z = move(x, y, z)
        pairs += [(index_of(x, c, z, y), index_of(to_x, c, to_z, to_y)) for c in (0, 1)]
    return pairs


def total_of(half):
    core = 0
    running = half.astype(jnp.float32) + lax.ppermute(half, AXES, swap_cores()).astype(jnp.float32)
    for stage in STAGES:
        value = running.astype(jnp.bfloat16)
        near = [
            lax.ppermute(value, AXES, hand_over(core, move)).astype(jnp.float32)
            for move in (*stage, both(*stage))
        ]
        own = lax.ppermute(value, AXES, swap_cores()).astype(jnp.float32)
        running = (own + near[0]) + (near[1] + near[2])
        core = 1 - core
    value = running.astype(jnp.bfloat16)
    crossed = lax.ppermute(value, AXES, hand_over(core, LAST)).astype(jnp.float32)
    own = lax.ppermute(value, AXES, swap_cores()).astype(jnp.float32)
    total = (own + crossed).astype(jnp.bfloat16)
    other = lax.ppermute(total, AXES, swap_cores())
    return jnp.where(lax.axis_index("c") == core, other, total)


def mask_of(flat, rows):
    lane = lax.broadcasted_iota(jnp.int32, (rows, WIDTH), 1)
    return (lane >= flat * MODES) & (lane < (flat + 1) * MODES)


def dot(a, b, dims=((1,), (0,))):
    return lax.dot_general(a, b, (dims, ((), ())), preferred_element_type=jnp.float32)


def split(value):
    high = value.astype(jnp.bfloat16)
    return high, (value - high.astype(jnp.float32)).astype(jnp.bfloat16)


def where_am_i():
    gx = lax.axis_index("x") * 2 + lax.axis_index("c")
    gy = lax.axis_index("z") * 4 + lax.axis_index("y")
    return gx, gy


def analyse(
    scale, fields, x_tables, y_tables, x_wides, out, x_wide, y_table, blocks, x_table, high, low, sems
):
    gx, gy = where_am_i()
    copy_y = pltpu.make_async_copy(y_tables.at[gy, pl.ds(0, 2 * MODES)], y_table, sems.at[FLAT])
    copy_x = pltpu.make_async_copy(x_tables.at[gx, pl.ds(0, MODES)], x_table, sems.at[FLAT + 1])
    copy_wide = pltpu.make_async_copy(x_wides.at[gx], x_wide, sems.at[FLAT + 2])
    copies = [
        pltpu.make_async_copy(fields.at[f], blocks.at[pl.ds(2 * f, 2)], sems.at[f])
        for f in range(FLAT // 2)
    ]
    copies[0].start()
    copy_x.start()
    copy_y.start()
    for copy in copies[1:]:
        copy.start()
    copy_wide.start()
    copy_y.wait()
    y_high = jnp.concatenate([y_table[:MODES]] * FLAT)
    y_low = jnp.concatenate([y_table[MODES:]] * FLAT)
    copy_x.wait()
    for pair in range(0, FLAT, 2):
        copies[pair // 2].wait()
        for f in (pair, pair + 1):
            mine = pl.ds(f * MODES, MODES)
            high[mine], low[mine] = split(dot(x_table[...], blocks[f]))
    last = ((1,), (1,))
    product = (
        dot(high[...], y_high, last) + dot(low[...], y_high, last) + dot(high[...], y_low, last)
    )
    total = jnp.zeros((MODES, WIDTH), jnp.float32)
    for f in range(FLAT):
        total = jnp.where(mask_of(f, MODES), product[f * MODES : (f + 1) * MODES], total)
    out[...] = (total * scale).astype(jnp.bfloat16)
    copy_wide.wait()


def synthesise(sums, parent, rate, x_table, y_table, out, spectra, blocks, modes, sems):
    y_high, y_low = y_table[:MODES], y_table[MODES:]
    p_high, p_low = split(jnp.concatenate([parent[f // 2, f % 2] for f in range(FLAT)]))
    wanted = dot(p_high, y_high) + dot(p_low, y_high) + dot(p_high, y_low)
    high = sums[...]
    none = jnp.zeros((MODES, WIDTH), jnp.bfloat16)
    highs = jnp.concatenate([jnp.where(mask_of(f, MODES), high, none) for f in range(FLAT)])
    y_high, y_low = jnp.concatenate([y_high] * FLAT), jnp.concatenate([y_low] * FLAT)
    found = dot(highs, y_high) + dot(highs, y_low)
    row = lax.broadcasted_iota(jnp.int32, (WIDTH, MODES), 0)
    mode = lax.broadcasted_iota(jnp.int32, (WIDTH, MODES), 1)
    gather = (row % MODES == mode).astype(jnp.bfloat16)
    copies = []
    for f in range(FLAT):
        mine = slice(f * MODES, (f + 1) * MODES)
        pull = rate[f // 2 : f // 2 + 1, f % 2 : f % 2 + 1] / MODES
        a_high, a_low = split(pull * (wanted[mine] - found[mine]))
        weights = jnp.concatenate([a_high, a_high, a_low])
        blocks[f] = dot(x_table[...], weights).astype(jnp.bfloat16)
        copies.append(pltpu.make_async_copy(blocks.at[f], out.at[f // 2, f % 2], sems.at[f]))
        copies[-1].start()
        if f == SPECTRA_AFTER:
            coeffs = dot(highs, gather)
            for g in range(FLAT):
                modes[g // 2, g % 2] = coeffs[g * MODES : (g + 1) * MODES]
            copies.append(pltpu.make_async_copy(modes, spectra, sems.at[FLAT]))
            copies[-1].start()
    for copy in copies:
        copy.wait()


def solution(mesh):
    fine = Mesh(mesh.devices.reshape(tuple(SIZES[a] for a in AXES)), AXES)
    total_x, total_y = 6144, 8192
    cols_x, cols_y = total_x // 8, total_y // 32
    x_high, x_low = halves(basis(total_x))
    y_high, y_low = halves(basis(total_y))
    narrow = np.pad(x_high.reshape(8, cols_x, MODES).transpose(0, 2, 1), ((0, 0), (0, 208), (0, 0)))
    x_wides = np.concatenate([x_high, x_low, x_high], 1).reshape(8, cols_x, 3 * MODES)
    y_tables = np.concatenate(
        [t.reshape(32, cols_y, MODES).transpose(0, 2, 1) for t in (y_high, y_low)], 1
    )
    y_tables = np.pad(y_tables, ((0, 0), (0, 96), (0, 0)))
    scale = 2.0 / math.sqrt(total_x * total_y)
    any_space = pl.BlockSpec(memory_space=pl.ANY)
    vmem = pl.BlockSpec(memory_space=pltpu.VMEM)
    small = jax.ShapeDtypeStruct((MODES, WIDTH), jnp.bfloat16)

    def per_device(fields, parent, rate):
        partial, x_wide, y_table = pl.pallas_call(
            lambda *refs: analyse(scale, *refs),
            out_shape=(
                small,
                jax.ShapeDtypeStruct((cols_x, 3 * MODES), jnp.bfloat16),
                jax.ShapeDtypeStruct((2 * MODES, cols_y), jnp.bfloat16),
            ),
            in_specs=[any_space] * 4,
            out_specs=(vmem, vmem, vmem),
            scratch_shapes=[
                pltpu.VMEM((FLAT, cols_x, cols_y), jnp.bfloat16),
                pltpu.VMEM((MODES, cols_x), jnp.bfloat16),
                pltpu.VMEM((FLAT * MODES, cols_y), jnp.bfloat16),
                pltpu.VMEM((FLAT * MODES, cols_y), jnp.bfloat16),
                pltpu.SemaphoreType.DMA((FLAT + 3,)),
            ],
            compiler_params=pltpu.CompilerParams(vmem_limit_bytes=52 << 20),
            name="analyse",
        )(fields, jnp.asarray(narrow), jnp.asarray(y_tables), jnp.asarray(x_wides))
        with jax.named_scope("total"):
            sums = total_of(partial)
        return pl.pallas_call(
            synthesise,
            out_shape=(
                jax.ShapeDtypeStruct((4, 2, cols_x, cols_y), jnp.bfloat16),
                jax.ShapeDtypeStruct((4, 2, MODES, MODES), jnp.float32),
            ),
            in_specs=[vmem] * 5,
            out_specs=(any_space, any_space),
            scratch_shapes=[
                pltpu.VMEM((FLAT, cols_x, cols_y), jnp.bfloat16),
                pltpu.VMEM((4, 2, MODES, MODES), jnp.float32),
                pltpu.SemaphoreType.DMA((FLAT + 1,)),
            ],
            compiler_params=pltpu.CompilerParams(vmem_limit_bytes=16 << 20),
            name="synthesise",
        )(sums, parent, rate, x_wide, y_table)

    grid = P(None, None, ("x", "c"), ("z", "y"))
    return jax.shard_map(
        per_device, mesh=fine, in_specs=(grid, P(), P()), out_specs=(grid, P()), check_vma=False
    )
```

```python
import math

import jax
import jax.numpy as jnp
import ml_dtypes
import numpy as np
from jax import lax
from jax.experimental import pallas as pl
from jax.experimental.pallas import tpu as pltpu
from jax.sharding import Mesh
from jax.sharding import PartitionSpec as P

KW = 24
MODES = 2 * KW
FLAT = 8
WIDTH = FLAT * MODES
SPECTRA_AFTER = 3
AXES = ("x", "c", "z", "y")
SIZES = {"x": 4, "c": 2, "z": 8, "y": 4}
CHIPS = [(x, y, z) for x in range(4) for y in range(4) for z in range(8)]


def basis(total):
    positions = np.arange(total, dtype=np.int64)
    modes = np.arange(MODES)
    wavenum = np.where(modes < KW, modes, modes - KW + 1)
    phase = (positions[:, None] * wavenum[None, :] % total) * (2.0 * math.pi / total)
    return np.where(modes[None, :] < KW, np.cos(phase), np.sin(phase)).astype(np.float32)


def halves(table):
    high = table.astype(ml_dtypes.bfloat16)
    low = (table - high.astype(np.float32)).astype(ml_dtypes.bfloat16)
    return high, low


def index_of(x, c, z, y):
    return ((x * 2 + c) * 8 + z) * 4 + y


def swap_cores():
    return [
        (index_of(x, c, z, y), index_of(x, 1 - c, z, y)) for x, y, z in CHIPS for c in (0, 1)
    ]


def hand_over(core, move):
    pairs = []
    for x, y, z in CHIPS:
        to_x, to_y, to_z = move(x, y, z)
        pairs.append((index_of(x, core, z, y), index_of(to_x, 1 - core, to_z, to_y)))
        pairs.append((index_of(x, 1 - core, z, y), index_of(x, core, z, y)))
    return pairs


def both(first, second):
    return lambda x, y, z: second(*first(x, y, z))


FLIP_X0 = lambda x, y, z: (x ^ 1, y, z)
FLIP_X1 = lambda x, y, z: (3 - x, y, z)
FLIP_Y0 = lambda x, y, z: (x, y ^ 1, z)
FLIP_Y1 = lambda x, y, z: (x, 3 - y, z)
FLIP_Z0 = lambda x, y, z: (x, y, z ^ 1)
FLIP_Z1 = lambda x, y, z: (x, y, z ^ 2)
FLIP_Z2 = lambda x, y, z: (x, y, 7 - z)
STAGES = ((FLIP_X0, FLIP_Y0), (FLIP_Z0, FLIP_Z1), (FLIP_X1, FLIP_Y1))
LAST = FLIP_Z2


def on_both(move):
    pairs = []
    for x, y, z in CHIPS:
        to_x, to_y, to_z = move(x, y, z)
        pairs += [(index_of(x, c, z, y), index_of(to_x, c, to_z, to_y)) for c in (0, 1)]
    return pairs


def total_of(half):
    core = 0
    running = half.astype(jnp.float32) + lax.ppermute(half, AXES, swap_cores()).astype(jnp.float32)
    for stage in STAGES:
        value = running.astype(jnp.bfloat16)
        near = [
            lax.ppermute(value, AXES, hand_over(core, move)).astype(jnp.float32)
            for move in (*stage, both(*stage))
        ]
        own = lax.ppermute(value, AXES, swap_cores()).astype(jnp.float32)
        running = (own + near[0]) + (near[1] + near[2])
        core = 1 - core
    value = running.astype(jnp.bfloat16)
    crossed = lax.ppermute(value, AXES, hand_over(core, LAST)).astype(jnp.float32)
    own = lax.ppermute(value, AXES, swap_cores()).astype(jnp.float32)
    total = (own + crossed).astype(jnp.bfloat16)
    other = lax.ppermute(total, AXES, swap_cores())
    return jnp.where(lax.axis_index("c") == core, other, total)


def mask_of(flat, rows):
    lane = lax.broadcasted_iota(jnp.int32, (rows, WIDTH), 1)
    return (lane >= flat * MODES) & (lane < (flat + 1) * MODES)


def dot(a, b, dims=((1,), (0,))):
    return lax.dot_general(a, b, (dims, ((), ())), preferred_element_type=jnp.float32)


def split(value):
    high = value.astype(jnp.bfloat16)
    return high, (value - high.astype(jnp.float32)).astype(jnp.bfloat16)


def where_am_i():
    gx = lax.axis_index("x") * 2 + lax.axis_index("c")
    gy = lax.axis_index("z") * 4 + lax.axis_index("y")
    return gx, gy


def analyse(
    scale, fields, x_tables, y_tables, x_wides, out, x_wide, y_table, blocks, x_table, high, low, sems
):
    gx, gy = where_am_i()
    copy_y = pltpu.make_async_copy(y_tables.at[gy, pl.ds(0, 2 * MODES)], y_table, sems.at[FLAT])
    copy_x = pltpu.make_async_copy(x_tables.at[gx, pl.ds(0, MODES)], x_table, sems.at[FLAT + 1])
    copy_wide = pltpu.make_async_copy(x_wides.at[gx], x_wide, sems.at[FLAT + 2])
    copies = [
        pltpu.make_async_copy(fields.at[f], blocks.at[pl.ds(2 * f, 2)], sems.at[f])
        for f in range(FLAT // 2)
    ]
    copies[0].start()
    copy_x.start()
    copy_y.start()
    for copy in copies[1:]:
        copy.start()
    copy_wide.start()
    copy_y.wait()
    y_high, y_low = y_table[:MODES], y_table[MODES:]
    copy_x.wait()
    for pair in range(0, FLAT, 2):
        copies[pair // 2].wait()
        for f in (pair, pair + 1):
            mine = pl.ds(f * MODES, MODES)
            high[mine], low[mine] = split(dot(x_table[...], blocks[f]))
    last = ((1,), (1,))
    product = (
        dot(high[...], y_high, last) + dot(low[...], y_high, last) + dot(high[...], y_low, last)
    )
    total = jnp.concatenate([product[f * MODES : (f + 1) * MODES] for f in range(FLAT)], 1)
    out[...] = (total * scale).astype(jnp.bfloat16)
    copy_wide.wait()


def synthesise(sums, parent, rate, x_table, y_table, out, spectra, blocks, modes, sems):
    y_high, y_low = y_table[:MODES], y_table[MODES:]
    p_high, p_low = split(jnp.concatenate([parent[f // 2, f % 2] for f in range(FLAT)]))
    wanted = dot(p_high, y_high) + dot(p_low, y_high) + dot(p_high, y_low)
    high = sums[...]
    none = jnp.zeros((MODES, WIDTH), jnp.bfloat16)
    highs = jnp.concatenate([jnp.where(mask_of(f, MODES), high, none) for f in range(FLAT)])
    y_high, y_low = jnp.concatenate([y_high] * FLAT), jnp.concatenate([y_low] * FLAT)
    found = dot(highs, y_high) + dot(highs, y_low)
    row = lax.broadcasted_iota(jnp.int32, (WIDTH, MODES), 0)
    mode = lax.broadcasted_iota(jnp.int32, (WIDTH, MODES), 1)
    gather = (row % MODES == mode).astype(jnp.bfloat16)
    copies = []
    for f in range(FLAT):
        mine = slice(f * MODES, (f + 1) * MODES)
        pull = rate[f // 2 : f // 2 + 1, f % 2 : f % 2 + 1] / MODES
        a_high, a_low = split(pull * (wanted[mine] - found[mine]))
        weights = jnp.concatenate([a_high, a_high, a_low])
        blocks[f] = dot(x_table[...], weights).astype(jnp.bfloat16)
        copies.append(pltpu.make_async_copy(blocks.at[f], out.at[f // 2, f % 2], sems.at[f]))
        copies[-1].start()
        if f == SPECTRA_AFTER:
            coeffs = dot(highs, gather)
            for g in range(FLAT):
                modes[g // 2, g % 2] = coeffs[g * MODES : (g + 1) * MODES]
            copies.append(pltpu.make_async_copy(modes, spectra, sems.at[FLAT]))
            copies[-1].start()
    for copy in copies:
        copy.wait()


def solution(mesh):
    fine = Mesh(mesh.devices.reshape(tuple(SIZES[a] for a in AXES)), AXES)
    total_x, total_y = 6144, 8192
    cols_x, cols_y = total_x // 8, total_y // 32
    x_high, x_low = halves(basis(total_x))
    y_high, y_low = halves(basis(total_y))
    narrow = np.pad(x_high.reshape(8, cols_x, MODES).transpose(0, 2, 1), ((0, 0), (0, 208), (0, 0)))
    x_wides = np.concatenate([x_high, x_low, x_high], 1).reshape(8, cols_x, 3 * MODES)
    y_tables = np.concatenate(
        [t.reshape(32, cols_y, MODES).transpose(0, 2, 1) for t in (y_high, y_low)], 1
    )
    y_tables = np.pad(y_tables, ((0, 0), (0, 96), (0, 0)))
    scale = 2.0 / math.sqrt(total_x * total_y)
    any_space = pl.BlockSpec(memory_space=pl.ANY)
    vmem = pl.BlockSpec(memory_space=pltpu.VMEM)
    small = jax.ShapeDtypeStruct((MODES, WIDTH), jnp.bfloat16)

    def per_device(fields, parent, rate):
        partial, x_wide, y_table = pl.pallas_call(
            lambda *refs: analyse(scale, *refs),
            out_shape=(
                small,
                jax.ShapeDtypeStruct((cols_x, 3 * MODES), jnp.bfloat16),
                jax.ShapeDtypeStruct((2 * MODES, cols_y), jnp.bfloat16),
            ),
            in_specs=[any_space] * 4,
            out_specs=(vmem, vmem, vmem),
            scratch_shapes=[
                pltpu.VMEM((FLAT, cols_x, cols_y), jnp.bfloat16),
                pltpu.VMEM((MODES, cols_x), jnp.bfloat16),
                pltpu.VMEM((FLAT * MODES, cols_y), jnp.bfloat16),
                pltpu.VMEM((FLAT * MODES, cols_y), jnp.bfloat16),
                pltpu.SemaphoreType.DMA((FLAT + 3,)),
            ],
            compiler_params=pltpu.CompilerParams(vmem_limit_bytes=52 << 20),
            name="analyse",
        )(fields, jnp.asarray(narrow), jnp.asarray(y_tables), jnp.asarray(x_wides))
        with jax.named_scope("total"):
            sums = total_of(partial)
        return pl.pallas_call(
            synthesise,
            out_shape=(
                jax.ShapeDtypeStruct((4, 2, cols_x, cols_y), jnp.bfloat16),
                jax.ShapeDtypeStruct((4, 2, MODES, MODES), jnp.float32),
            ),
            in_specs=[vmem] * 5,
            out_specs=(any_space, any_space),
            scratch_shapes=[
                pltpu.VMEM((FLAT, cols_x, cols_y), jnp.bfloat16),
                pltpu.VMEM((4, 2, MODES, MODES), jnp.float32),
                pltpu.SemaphoreType.DMA((FLAT + 1,)),
            ],
            compiler_params=pltpu.CompilerParams(vmem_limit_bytes=16 << 20),
            name="synthesise",
        )(sums, parent, rate, x_wide, y_table)

    grid = P(None, None, ("x", "c"), ("z", "y"))
    return jax.shard_map(
        per_device, mesh=fine, in_specs=(grid, P(), P()), out_specs=(grid, P()), check_vma=False
    )
```
